32 devices in a mesh: req: 8 (over z, x), tp: 4 (over y, core).
Axes of the slice: x: 2, y: 2, z: 4, core: 2. Of those that a mesh axis runs over, the one named last changes fastest.
Arguments:
- x_pre: bfloat16 [4096, 1280], P('req', 'tp'), may hold values from -6 to 6
- x_dec: bfloat16 [32, 1280], P('req', 'tp'), may hold values from -6 to 6
- norm_gain: float32 [1280], replicated, may hold values from 0.1 to 1.9
- w_qkv: bfloat16 [3, 1280, 1280], P(None, None, 'tp'), may hold values from -0.15625 to 0.15625
- w_out: bfloat16 [1280, 1280], P('tp'), may hold values from -0.625 to 0.625
- pre_keys: bfloat16 [3072, 1280], P('req', 'tp'), may hold values from -70 to 70
- pre_values: bfloat16 [3072, 1280], P('req', 'tp'), may hold values from -6 to 6
- pre_lens: int32 [8], P('req'), may hold values from 0 to 384, as said below
- dec_keys: bfloat16 [5120, 1280], P('req', 'tp'), may hold values from -70 to 70
- dec_values: bfloat16 [5120, 1280], P('req', 'tp'), may hold values from -6 to 6
- dec_lens: int32 [32], replicated, may hold values from 1 to 3200, as said below
Outputs:
- pre_out: bfloat16 [4096, 1280], P('req', 'tp')
- dec_out: bfloat16 [32, 1280], P('req', 'tp')
The draws below stay inside these ranges and needn't reach their ends.
Inputs may be any that keep to these rules, and one draw needn't show every extreme that they name: `pre_lens`: at least one prefill block has all 384 cached rows valid. `dec_lens`: the lengths sum to 3840; request 0 has exactly 3200 rows, every other request fewer.
All inputs are finite; a program needn't handle non-finite values.
Results may differ from the reference program's by a relative error of at most 0.012.
The reference program's roundings to bfloat16 on the way count: a program that leaves them out, or rounds other values in their place, can miss the bound.
Values may be sent and summed in bfloat16 or wider, within the bound.
A program may use at most 64 MiB of HBM per device.

```python
import math
import jax
import jax.numpy as jnp
from jax import lax

D = 1280
H = 16
HD = 80
PRE_DEV = 512
PREF = 384
PRE = 4096
PREFIX = 3072
DEC = 32
POOL = 5120
MAXLEN = 3200
FILLED = 3840
N_REQ = 8


def spiky_keys(key, rows):
    base = jnp.clip(jax.random.normal(key, (rows, D), jnp.float32), -6.0, 6.0)
    return base.astype(jnp.bfloat16)


def draw_pre_keys(key, part):
    return spiky_keys(jax.random.fold_in(key, 3), PREFIX)


def draw_dec_keys(key, part):
    return spiky_keys(jax.random.fold_in(key, 5), POOL)


def draw_pre_lens(key, part):
    count = PREFIX // PREF
    first_key = jax.random.fold_in(key, 7)
    second_key = jax.random.fold_in(key, 9)
    lengths = jax.random.randint(first_key, (count,), 0, PREF + 1)
    full_place = jax.random.randint(second_key, (), 0, count)
    return jnp.where(jnp.arange(count) == full_place, PREF, lengths).astype(jnp.int32)


def draw_dec_lens(key, part):
    others = DEC - 1
    extra = FILLED - MAXLEN - others
    cut_key = jax.random.fold_in(key, 13)
    cuts = jnp.sort(jax.random.randint(cut_key, (others - 1,), 0, extra + 1))
    edges = jnp.concatenate([jnp.zeros((1,), jnp.int32), cuts.astype(jnp.int32), jnp.full((1,), extra, jnp.int32)])
    rest = (edges[1:] - edges[:-1] + 1).astype(jnp.int32)
    return jnp.concatenate([jnp.full((1,), MAXLEN, jnp.int32), rest]).astype(jnp.int32)


def shard_levels(own_key, dims, pieces, smallest, largest):
    loudness, own = 1.0, jax.random.fold_in(own_key, 6)
    for axis_at, parts in pieces:
        steps = jnp.exp(jax.random.uniform(jax.random.fold_in(own, axis_at), (parts,), jnp.float32, smallest / len(pieces), largest / len(pieces)))
        loudness = loudness * jnp.repeat(steps, dims[axis_at] // parts).reshape([-1 if axis == axis_at else 1 for axis in range(len(dims))])
    return loudness


def gaussian(key, extent, deviation, most, split=(), held_as=jnp.bfloat16):
    drawn = jax.random.normal(key, extent, jnp.float32) * deviation
    if len(split) > 0:
        drawn = shard_levels(key, extent, split, -0.22, 0.18) * drawn
    return jnp.clip(drawn, min=-most, max=most).astype(held_as)


def setup_inputs(seed: int = 0) -> dict:
    keys = jax.random.split(jax.random.key(seed), 12)
    return {
        "x_pre": gaussian(keys[0], (PRE, D), 1.0, 6.0, ((0, 8), (1, 4))),
        "x_dec": gaussian(keys[1], (DEC, D), 1.0, 6.0, ((0, 8), (1, 4))),
        "norm_gain": jnp.clip(1.0 + 0.18 * jax.random.normal(keys[2], (D,), jnp.float32), 0.1, 1.9),
        "w_qkv": gaussian(keys[3], (3, D, D), D ** -0.5, 0.15625, ((2, 4),)),
        "w_out": gaussian(keys[4], (D, D), HD ** -0.5, 0.625, ((0, 4),)),
        "pre_keys": draw_pre_keys(jax.random.fold_in(keys[11], 71), 0),
        "pre_values": gaussian(keys[6], (PREFIX, D), 1.0, 6.0, ((0, 8), (1, 4))),
        "pre_lens": draw_pre_lens(jax.random.fold_in(keys[11], 71), 0),
        "dec_keys": draw_dec_keys(jax.random.fold_in(keys[11], 71), 0),
        "dec_values": gaussian(keys[9], (POOL, D), 1.0, 6.0, ((0, 8), (1, 4))),
        "dec_lens": draw_dec_lens(jax.random.fold_in(keys[11], 71), 0),
    }


EPSILON = 1e-06
MASKED_SCORE = -1e+30

def normalize(tokens, norm_gain):
    tokens_f = tokens.astype(jnp.float32)
    mean_square = lax.optimization_barrier(jnp.mean(tokens_f * tokens_f, axis=-1, keepdims=True))
    return (tokens_f * lax.rsqrt(mean_square + EPSILON) * norm_gain.astype(jnp.float32)).astype(jnp.bfloat16)

def project(hidden, w_qkv):
    return tuple((jnp.dot(hidden, w_qkv[matrix_index], preferred_element_type=jnp.float32).astype(jnp.bfloat16) for matrix_index in range(3)))

def rounded(weights):
    held = lax.optimization_barrier(weights.astype(jnp.bfloat16))
    return held.astype(jnp.float32)

def prefill_block(block_items):
    queries, keys_new, values_new, cache_keys, cache_values, prefix = block_items
    score_scale = 1.0 / math.sqrt(HD)
    keys_all = jnp.concatenate([cache_keys, keys_new], axis=0).astype(jnp.float32).reshape(-1, H, HD)
    values_all = jnp.concatenate([cache_values, values_new], axis=0).astype(jnp.float32).reshape(-1, H, HD)
    query_f = queries.astype(jnp.float32).reshape(-1, H, HD)
    scores = jnp.einsum('phd,rhd->hpr', query_f, keys_all) * score_scale
    column = jnp.arange(keys_all.shape[0], dtype=jnp.int32)[None, :]
    position = jnp.arange(query_f.shape[0], dtype=jnp.int32)[:, None]
    cached = cache_keys.shape[0]
    allowed = jnp.where(column < cached, column < prefix, column - cached <= position)
    scores = jnp.where(allowed[None], scores, MASKED_SCORE)
    row_top = lax.optimization_barrier(jnp.max(scores, axis=-1, keepdims=True))
    weights = jnp.where(allowed[None], jnp.exp(scores - row_top), 0.0)
    totals = lax.optimization_barrier(jnp.sum(weights, axis=-1))
    mixed = jnp.einsum('hpr,rhd->hpd', rounded(weights), values_all) / totals[..., None]
    return jnp.transpose(mixed, (1, 0, 2)).reshape(query_f.shape[0], D).astype(jnp.bfloat16)

def reference(x_pre, x_dec, norm_gain, w_qkv, w_out, pre_keys, pre_values, pre_lens, dec_keys, dec_values, dec_lens):
    score_scale = 1.0 / math.sqrt(HD)
    query_pre, key_pre, value_pre = project(normalize(x_pre, norm_gain), w_qkv)
    attn_pre = lax.map(prefill_block, (query_pre.reshape(N_REQ, PRE_DEV, D), key_pre.reshape(N_REQ, PRE_DEV, D), value_pre.reshape(N_REQ, PRE_DEV, D), pre_keys.reshape(N_REQ, PREF, D), pre_values.reshape(N_REQ, PREF, D), pre_lens))
    attn_pre = attn_pre.reshape(PRE, D)
    query_dec, key_dec, value_dec = project(normalize(x_dec, norm_gain), w_qkv)
    starts = (jnp.cumsum(dec_lens) - dec_lens).astype(jnp.int32)
    padding = jnp.zeros((MAXLEN, D), jnp.bfloat16)
    keys_pad = jnp.concatenate([dec_keys, padding], axis=0)
    values_pad = jnp.concatenate([dec_values, padding], axis=0)

    def decode_one(request_items):
        query, key_self, value_self, row_start, length = request_items
        cache_k = lax.dynamic_slice_in_dim(keys_pad, row_start.astype(jnp.int32), MAXLEN, 0).astype(jnp.float32).reshape(MAXLEN, H, HD)
        cache_v = lax.dynamic_slice_in_dim(values_pad, row_start.astype(jnp.int32), MAXLEN, 0).astype(jnp.float32).reshape(MAXLEN, H, HD)
        query_f = query.astype(jnp.float32).reshape(H, HD)
        scores = jnp.einsum('hd,rhd->hr', query_f, cache_k) * score_scale
        self_score = lax.optimization_barrier(jnp.sum(query_f * key_self.astype(jnp.float32).reshape(H, HD), axis=-1)) * score_scale
        allowed = jnp.arange(MAXLEN, dtype=jnp.int32) < length
        scores = jnp.where(allowed[None], scores, MASKED_SCORE)
        row_top = jnp.maximum(lax.optimization_barrier(jnp.max(scores, axis=-1)), self_score)
        weights = jnp.where(allowed[None], jnp.exp(scores - row_top[:, None]), 0.0)
        self_weight = jnp.exp(self_score - row_top)
        numerator = jnp.einsum('hr,rhd->hd', rounded(weights), cache_v) + rounded(self_weight)[:, None] * value_self.astype(jnp.float32).reshape(H, HD)
        denominator = lax.optimization_barrier(jnp.sum(weights, axis=-1)) + self_weight
        return (numerator / denominator[:, None]).reshape(D).astype(jnp.bfloat16)
    attn_dec = lax.map(decode_one, (query_dec, key_dec, value_dec, starts, dec_lens))
    pre_out = jnp.dot(attn_pre, w_out, preferred_element_type=jnp.float32).astype(jnp.bfloat16)
    dec_out = jnp.dot(attn_dec, w_out, preferred_element_type=jnp.float32).astype(jnp.bfloat16)
    return (pre_out, dec_out)
```

```python
import functools
import math

import jax
import jax.numpy as jnp
from jax import lax
from jax.experimental import pallas as pl
from jax.experimental.pallas import tpu as pltpu
from jax.sharding import PartitionSpec as P

HD = 80
EPSILON = 1e-06
MASKED = -1e30
CHUNK = 128
DEC_ROWS = 8
EXP_SCALE = math.log2(math.e) / math.sqrt(HD)
WINDOWS = ((0, 128), (0, 256), (128, 256), (128, 320))
F32, BF16 = jnp.float32, jnp.bfloat16


def lanes(shape, start=0):
    return lax.broadcasted_iota(jnp.int32, shape, len(shape) - 1) + start


def head_lanes(block, head):
    low, high = WINDOWS[head]
    part = block[:, low:high]
    lane = lanes(part.shape, low)
    return jnp.where((lane >= head * HD) & (lane < (head + 1) * HD), part, 0.0)


def join_heads(parts):
    lane = lanes((parts[0].shape[0], 128))
    first = jnp.where(lane < HD, parts[0], parts[1][:, :128])
    second = jnp.where(
        lane < 2 * HD - 128, parts[1][:, 128:], jnp.where(lane < 3 * HD - 128, parts[2], parts[3][:, :128])
    )
    return jnp.concatenate([first, second, parts[3][:, 128:]], axis=1)


def spread(columns, shape):
    lane = lanes(shape)
    out = jnp.broadcast_to(columns[3], shape)
    for head in (2, 1, 0):
        out = jnp.where(lane < (head + 1) * HD, columns[head], out)
    return out


def dot(a, b):
    return jnp.dot(a, b, preferred_element_type=F32)


def dot_nt(a, b):
    return lax.dot_general(a, b, (((1,), (1,)), ((), ())), preferred_element_type=F32)


def each(count, step):
    if count <= 16:
        for k in range(1, count):
            step(k)
    else:

        def loop(k, carry):
            step(k)
            return carry

        lax.fori_loop(1, count, loop, 0)


def kernel(
    n,
    x_pre,
    x_dec,
    gain,
    w_qkv,
    w_out,
    pre_keys,
    pre_values,
    pre_lens,
    dec_keys,
    dec_values,
    dec_lens,
    out_pre,
    out_dec,
    xg,
    xdg,
    wq,
    wo,
    wsel,
    kall,
    vall,
    dk,
    dv,
    qg,
    part,
    pr,
    att,
    attd,
    own,
    psend,
    precv,
    ownd,
    pdsend,
    pdrecv,
    load_sem,
    xy_sem,
    xc_sem,
    xf_sem,
    wo_sem,
    q_sem,
    p_sem,
    a_sem,
    o_sem,
):
    rows = x_pre.shape[0]
    cached = pre_keys.shape[0]
    pool = dec_keys.shape[0]
    width = x_pre.shape[1]
    own_rows = x_dec.shape[0]
    chunks = rows // CHUNK
    me = lax.axis_index("req")
    t = lax.axis_index("tp")
    core = lax.rem(t, 2)
    half = lax.div(t, 2)
    mate = t + 1 - 2 * core
    across = lax.rem(t + 2, 4)

    def remote(src, dst, sems, at, where):
        return pltpu.make_async_remote_copy(
            src_ref=src,
            dst_ref=dst,
            send_sem=sems.at[0, at],
            recv_sem=sems.at[1, at],
            device_id=where,
            device_id_type=pl.DeviceIdType.MESH,
        )

    def chunk(i):
        return pl.ds(i * CHUNK, CHUNK)

    load_x = pltpu.make_async_copy(x_pre, xg.at[t], load_sem.at[0])
    load_wq = pltpu.make_async_copy(w_qkv, wq, load_sem.at[1])
    load_pk = pltpu.make_async_copy(pre_keys, kall.at[pl.ds(0, cached)], load_sem.at[2])
    load_pv = pltpu.make_async_copy(pre_values, vall.at[pl.ds(0, cached)], load_sem.at[3])
    load_dk = pltpu.make_async_copy(dec_keys, dk, load_sem.at[4])
    load_dv = pltpu.make_async_copy(dec_values, dv, load_sem.at[5])
    load_wo = pltpu.make_async_copy(w_out, wo.at[core], load_sem.at[6])
    load_x.start()
    load_wq.start()
    load_pk.start()
    load_pv.start()

    barrier = pltpu.get_barrier_semaphore()
    for peer in (mate, across):
        pl.semaphore_signal(barrier, inc=1, device_id={"tp": peer}, device_id_type=pl.DeviceIdType.MESH)

    def greet(k):
        pl.semaphore_signal(
            barrier, inc=1, device_id={"req": lax.rem(me + k, n)}, device_id_type=pl.DeviceIdType.MESH
        )

    each(n, greet)
    dec_own = x_dec[...].astype(F32)
    xdg[t] = jnp.zeros((DEC_ROWS, width), F32)
    xdg[t, 0:own_rows] = dec_own
    pl.semaphore_wait(barrier, n + 1)

    def x_copies(sems, where, owner):
        copies = [remote(xdg.at[owner], xdg.at[owner], sems, chunks, where)]
        for i in range(chunks):
            src = x_pre.at[chunk(i)] if owner is t else xg.at[owner, chunk(i)]
            copies.append(remote(src, xg.at[owner, chunk(i)], sems, i, where))
        return copies

    over = x_copies(xy_sem, {"tp": across}, t)
    beside = x_copies(xc_sem, {"tp": mate}, t)
    passed = x_copies(xf_sem, {"tp": mate}, across)
    for i in range(chunks + 1):
        over[i].start()
    for i in range(chunks + 1):
        beside[i].start()
    load_wo.start()
    load_dk.start()
    load_dv.start()
    share_wo = remote(w_out, wo.at[core], wo_sem, 0, {"tp": mate})
    share_wo.start()

    def pass_on(i):
        over[i].wait_recv()
        passed[i].start()

    gain_row = gain[...]

    def normalize(pieces):
        tokens = jnp.concatenate(pieces, axis=1)
        mean_square = jnp.sum(tokens * tokens, axis=-1, keepdims=True) * (1.0 / tokens.shape[1])
        return tokens * lax.rsqrt(mean_square + EPSILON) * gain_row

    pass_on(0)
    pass_on(1)
    beside[0].wait_recv()
    passed[0].wait_recv()
    dec_normed = normalize([xdg[p] for p in range(4)])
    load_x.wait()

    prefix = pre_lens[0]
    prefix_bias = jnp.where(lanes((1, cached)) < prefix, 0.0, MASKED)
    tri = (CHUNK, CHUNK)
    causal_bias = jnp.where(lanes(tri) <= lax.broadcasted_iota(jnp.int32, tri, 0), 0.0, MASKED)

    def project(i):
        beside[i + 1].wait_recv()
        passed[i + 1].wait_recv()
        normed = normalize([xg[p, chunk(i)].astype(F32) for p in range(4)]).astype(BF16)
        if i == 0:
            extra = jnp.concatenate([dec_normed, dec_normed], axis=0).astype(BF16)
            normed = jnp.concatenate([normed, extra], axis=0)
            load_wq.wait()
        return [dot(normed, wq[m]).astype(BF16) for m in range(3)]

    def attend(i, query):
        seen = cached + (i + 1) * CHUNK
        parts = []
        for head in range(4):
            low, high = WINDOWS[head]
            q = head_lanes(query, head)
            scores = dot_nt(q, kall[0:seen, low:high])
            pieces = [scores[:, :cached] + prefix_bias]
            if i > 0:
                pieces.append(scores[:, cached : seen - CHUNK])
            pieces.append(scores[:, seen - CHUNK :] + causal_bias)
            scores = jnp.concatenate(pieces, axis=1)
            top = jnp.max(scores, axis=-1, keepdims=True)
            weights = jnp.exp2((scores - top) * EXP_SCALE)
            total = jnp.sum(weights, axis=-1, keepdims=True)
            parts.append(dot(weights.astype(BF16), vall[0:seen, low:high]) / total)
        att[core, chunk(i)] = join_heads(parts).astype(BF16)

    att_copies = [
        remote(att.at[core, chunk(i)], att.at[core, chunk(i)], a_sem, i, {"tp": mate}) for i in range(chunks)
    ]
    attd_copy = remote(attd.at[core], attd.at[core], a_sem, chunks, {"tp": mate})
    out_copies = [remote(psend.at[chunk(i)], precv.at[chunk(i)], o_sem, i, {"tp": across}) for i in range(chunks)]
    outd_copy = remote(pdsend, pdrecv, o_sem, chunks, {"tp": across})

    def out_terms(a, to):
        return dot(a[0], wsel[to, 0]) + dot(a[1], wsel[to, 1])

    def out_project(i, with_dec):
        att_copies[i].wait_recv()
        a = [att[c, chunk(i)] for c in range(2)]
        if with_dec:
            attd_copy.wait_recv()
            d = [attd[c] for c in range(2)]
            a = [
                jnp.concatenate([a[c], jnp.concatenate([d[c], d[c]], axis=0).astype(BF16)], axis=0)
                for c in range(2)
            ]
        sent = out_terms(a, 1 - half)
        psend[chunk(i)] = sent[:CHUNK].astype(BF16)
        out_copies[i].start()
        if with_dec:
            pdsend[...] = sent[CHUNK : CHUNK + DEC_ROWS]
            outd_copy.start()
        kept = out_terms(a, half)
        own[chunk(i)] = kept[:CHUNK]
        if with_dec:
            ownd[...] = kept[CHUNK : CHUNK + DEC_ROWS]

    def finish(i):
        out_copies[i].wait_recv()
        out_pre[chunk(i)] = (own[chunk(i)] + precv[chunk(i)].astype(F32)).astype(BF16)

    def q_copy(k):
        return remote(qg.at[me], qg.at[me], q_sem, k, {"req": lax.rem(me + k, n)})

    def p_copy(k):
        to = lax.rem(me + k, n)
        return remote(part.at[to], pr.at[me], p_sem, k, {"req": to})

    def decode_partials():
        each(n, lambda k: q_copy(k).wait_recv())
        load_dk.wait()
        load_dv.wait()
        queries = qg[...].reshape(n * DEC_ROWS, width).astype(BF16)
        lens = dec_lens[...].astype(F32)
        grid = (n * DEC_ROWS, lens.shape[1])
        row = lax.broadcasted_iota(jnp.int32, grid, 0)
        place = lax.rem(row, DEC_ROWS)
        request = lax.div(row, DEC_ROWS) * own_rows + place
        real = place < own_rows
        column = lanes(grid)
        start = jnp.sum(jnp.where(real & (column < request), lens, 0.0), axis=-1, keepdims=True)
        end = jnp.sum(jnp.where(real & (column <= request), lens, 0.0), axis=-1, keepdims=True)
        pool_row = (me * pool + lanes((1, pool))).astype(F32)
        allowed = (pool_row >= start) & (pool_row < end)
        parts = []
        stats = jnp.zeros((n * DEC_ROWS, 128), F32)
        stat_lane = lanes(stats.shape)
        for head in range(4):
            low, high = WINDOWS[head]
            scores = dot_nt(head_lanes(queries, head), dk[:, low:high])
            scores = jnp.where(allowed, scores, MASKED)
            top = jnp.max(scores, axis=-1, keepdims=True)
            weights = jnp.where(allowed, jnp.exp2((scores - top) * EXP_SCALE), 0.0)
            total = jnp.sum(weights, axis=-1, keepdims=True)
            parts.append(dot(weights.astype(BF16), dv[:, low:high]))
            stats = jnp.where(stat_lane == head, top, jnp.where(stat_lane == 4 + head, total, stats))
        part[:, :, 0:width] = join_heads(parts).reshape(n, DEC_ROWS, width)
        part[:, :, 384:512] = stats.reshape(n, DEC_ROWS, 128)
        each(n, lambda k: p_copy(k).start())
        pr[me] = part[me]

    def decode_combine(q, k, v):
        each(n, lambda j: p_copy(j).wait_recv())
        sums = pr[:, :, 0:width]
        stats = pr[:, :, 384:512]
        tops, totals, selves, factors = [], [], [], []
        product = q * k
        lane = lanes(product.shape)
        for head in range(4):
            inside = (lane >= head * HD) & (lane < (head + 1) * HD)
            self_score = jnp.sum(jnp.where(inside, product, 0.0), axis=-1, keepdims=True)
            local = stats[:, :, head : head + 1]
            top = jnp.maximum(jnp.max(local, axis=0), self_score)
            factor = jnp.exp2((local - top[None]) * EXP_SCALE)
            self_weight = jnp.exp2((self_score - top) * EXP_SCALE)
            totals.append(jnp.sum(factor * stats[:, :, 4 + head : 5 + head], axis=0) + self_weight)
            selves.append(self_weight.astype(BF16).astype(F32))
            factors.append(factor)
        mixed = jnp.sum(spread(factors, sums.shape) * sums, axis=0)
        mixed = mixed + spread(selves, v.shape) * v
        attd[core] = (mixed / spread(totals, v.shape)).astype(BF16).astype(F32)
        attd_copy.start()

    for i in range(chunks):
        q, k, v = project(i)
        at = pl.ds(cached + i * CHUNK, CHUNK)
        kall[at] = k[:CHUNK]
        vall[at] = v[:CHUNK]
        if i == 0:
            q_own, k_own, v_own = (a[CHUNK:].astype(F32)[:DEC_ROWS] for a in (q, k, v))
            qg[me] = q_own
            each(n, lambda j: q_copy(j).start())
            load_pk.wait()
            load_pv.wait()
        if i + 1 < chunks:
            pass_on(i + 2)
        attend(i, q[:CHUNK])
        att_copies[i].start()
        if i == 0:
            load_wo.wait()
            share_wo.wait_recv()
            for c in range(2):

                @pl.when(core == c)
                def _():
                    for to in range(2):
                        first = (2 * to + c) * width
                        for r in range(2):
                            wsel[to, r] = wo[r, :, first : first + width]

            decode_partials()
        if i == chunks - 2:
            decode_combine(q_own, k_own, v_own)
        if i > 0:
            out_project(i - 1, False)
    out_project(chunks - 1, True)
    for i in range(chunks):
        finish(i)
    outd_copy.wait_recv()
    out_dec[...] = (ownd[...] + pdrecv[...])[:own_rows].astype(BF16)

    for copy in over + beside + passed + [share_wo] + att_copies + [attd_copy] + out_copies + [outd_copy]:
        copy.wait_send()
    each(n, lambda k: q_copy(k).wait_send())
    each(n, lambda k: p_copy(k).wait_send())


def body(n, x_pre, x_dec, norm_gain, w_qkv, w_out, pre_keys, pre_values, pre_lens, dec_keys, dec_values, dec_lens):
    rows, width = x_pre.shape
    cached, pool = pre_keys.shape[0], dec_keys.shape[0]
    chunks = rows // CHUNK
    hbm = pl.BlockSpec(memory_space=pl.ANY)
    vmem = pl.BlockSpec(memory_space=pltpu.VMEM)
    smem = pl.BlockSpec(memory_space=pltpu.SMEM)
    dma = pltpu.SemaphoreType.DMA
    return pl.pallas_call(
        functools.partial(kernel, n),
        out_shape=(jax.ShapeDtypeStruct(x_pre.shape, BF16), jax.ShapeDtypeStruct(x_dec.shape, BF16)),
        in_specs=[hbm, vmem, vmem, hbm, hbm, hbm, hbm, smem, hbm, hbm, vmem],
        out_specs=(vmem, vmem),
        scratch_shapes=[
            pltpu.VMEM((4, rows, width), BF16),
            pltpu.VMEM((4, DEC_ROWS, width), F32),
            pltpu.VMEM(w_qkv.shape, BF16),
            pltpu.VMEM((2,) + w_out.shape, BF16),
            pltpu.VMEM((2, 2, width, width), BF16),
            pltpu.VMEM((cached + rows, width), BF16),
            pltpu.VMEM((cached + rows, width), BF16),
            pltpu.VMEM((pool, width), BF16),
            pltpu.VMEM((pool, width), BF16),
            pltpu.VMEM((n, DEC_ROWS, width), F32),
            pltpu.VMEM((n, DEC_ROWS, 512), F32),
            pltpu.VMEM((n, DEC_ROWS, 512), F32),
            pltpu.VMEM((2, rows, width), BF16),
            pltpu.VMEM((2, DEC_ROWS, width), F32),
            pltpu.VMEM((rows, width), F32),
            pltpu.VMEM((rows, width), BF16),
            pltpu.VMEM((rows, width), BF16),
            pltpu.VMEM((DEC_ROWS, width), F32),
            pltpu.VMEM((DEC_ROWS, width), F32),
            pltpu.VMEM((DEC_ROWS, width), F32),
            dma((7,)),
            dma((2, chunks + 1)),
            dma((2, chunks + 1)),
            dma((2, chunks + 1)),
            dma((2, 1)),
            dma((2, n)),
            dma((2, n)),
            dma((2, chunks + 1)),
            dma((2, chunks + 1)),
        ],
        compiler_params=pltpu.CompilerParams(
            collective_id=0, has_side_effects=True, vmem_limit_bytes=48 * 1024 * 1024
        ),
        cost_estimate=pl.CostEstimate(flops=4_000_000_000, bytes_accessed=6_000_000, transcendentals=2_000_000),
    )(
        x_pre,
        x_dec,
        norm_gain.reshape(1, -1),
        w_qkv,
        w_out,
        pre_keys,
        pre_values,
        pre_lens,
        dec_keys,
        dec_values,
        dec_lens.reshape(1, -1),
    )


def solution(mesh):
    return jax.shard_map(
        functools.partial(body, mesh.shape["req"]),
        mesh=mesh,
        in_specs=(
            P("req", "tp"),
            P("req", "tp"),
            P(),
            P(None, None, "tp"),
            P("tp", None),
            P("req", "tp"),
            P("req", "tp"),
            P("req"),
            P("req", "tp"),
            P("req", "tp"),
            P(),
        ),
        out_specs=(P("req", "tp"), P("req", "tp")),
        check_vma=False,
    )
```

```python
import functools
import math

import jax
import jax.numpy as jnp
from jax import lax
from jax.experimental import pallas as pl
from jax.experimental.pallas import tpu as pltpu
from jax.sharding import PartitionSpec as P

HD = 80
EPSILON = 1e-06
MASKED = -1e30
CHUNK = 128
DEC_ROWS = 8
EXP_SCALE = math.log2(math.e) / math.sqrt(HD)
WINDOWS = ((0, 128), (0, 256), (128, 256), (128, 320))
F32, BF16 = jnp.float32, jnp.bfloat16


def lanes(shape, start=0):
    return lax.broadcasted_iota(jnp.int32, shape, len(shape) - 1) + start


def head_lanes(block, head):
    low, high = WINDOWS[head]
    part = block[:, low:high]
    lane = lanes(part.shape, low)
    return jnp.where((lane >= head * HD) & (lane < (head + 1) * HD), part, 0.0)


def join_heads(parts):
    lane = lanes((parts[0].shape[0], 128))
    first = jnp.where(lane < HD, parts[0], parts[1][:, :128])
    second = jnp.where(
        lane < 2 * HD - 128, parts[1][:, 128:], jnp.where(lane < 3 * HD - 128, parts[2], parts[3][:, :128])
    )
    return jnp.concatenate([first, second, parts[3][:, 128:]], axis=1)


def spread(columns, shape):
    lane = lanes(shape)
    out = jnp.broadcast_to(columns[3], shape)
    for head in (2, 1, 0):
        out = jnp.where(lane < (head + 1) * HD, columns[head], out)
    return out


def dot(a, b):
    return jnp.dot(a, b, preferred_element_type=F32)


def dot_nt(a, b):
    return lax.dot_general(a, b, (((1,), (1,)), ((), ())), preferred_element_type=F32)


def each(count, step):
    if count <= 16:
        for k in range(1, count):
            step(k)
    else:

        def loop(k, carry):
            step(k)
            return carry

        lax.fori_loop(1, count, loop, 0)


def kernel(
    n,
    x_pre,
    x_dec,
    gain,
    w_qkv,
    w_out,
    pre_keys,
    pre_values,
    pre_lens,
    dec_keys,
    dec_values,
    dec_lens,
    out_pre,
    out_dec,
    xg,
    xdg,
    gain_t,
    wq,
    wo,
    wsel,
    kall,
    vall,
    dk,
    dv,
    qg,
    part,
    pr,
    att,
    attd,
    own,
    psend,
    precv,
    ownd,
    pdsend,
    pdrecv,
    load_sem,
    xy_sem,
    xc_sem,
    xf_sem,
    wo_sem,
    q_sem,
    p_sem,
    a_sem,
    o_sem,
):
    width, rows = x_pre.shape
    cached = pre_keys.shape[1]
    pool = dec_keys.shape[1]
    own_rows = x_dec.shape[0]
    chunks = rows // CHUNK
    me = lax.axis_index("req")
    t = lax.axis_index("tp")
    core = lax.rem(t, 2)
    half = lax.div(t, 2)
    mate = t + 1 - 2 * core
    across = lax.rem(t + 2, 4)

    def remote(src, dst, sems, at, where):
        return pltpu.make_async_remote_copy(
            src_ref=src,
            dst_ref=dst,
            send_sem=sems.at[0, at],
            recv_sem=sems.at[1, at],
            device_id=where,
            device_id_type=pl.DeviceIdType.MESH,
        )

    def chunk(i):
        return pl.ds(i * CHUNK, CHUNK)

    load_x = [
        pltpu.make_async_copy(x_pre.at[:, chunk(i)], xg.at[t, i], load_sem.at[6 + i]) for i in range(chunks)
    ]
    load_wq = pltpu.make_async_copy(w_qkv, wq, load_sem.at[1])
    load_pk = pltpu.make_async_copy(pre_keys, kall.at[:, pl.ds(0, cached)], load_sem.at[2])
    load_pv = pltpu.make_async_copy(pre_values, vall.at[:, pl.ds(0, cached)], load_sem.at[3])
    load_dk = pltpu.make_async_copy(dec_keys, dk, load_sem.at[4])
    load_dv = pltpu.make_async_copy(dec_values, dv, load_sem.at[5])
    load_wo = pltpu.make_async_copy(w_out, wo.at[core], load_sem.at[0])
    for i in range(chunks):
        load_x[i].start()
    load_wq.start()
    load_pk.start()
    load_pv.start()

    barrier = pltpu.get_barrier_semaphore()
    for peer in (mate, across):
        pl.semaphore_signal(barrier, inc=1, device_id={"tp": peer}, device_id_type=pl.DeviceIdType.MESH)

    def greet(k):
        pl.semaphore_signal(
            barrier, inc=1, device_id={"req": lax.rem(me + k, n)}, device_id_type=pl.DeviceIdType.MESH
        )

    each(n, greet)
    dec_own = x_dec[...].astype(F32)
    xdg[t] = jnp.zeros((DEC_ROWS, width), F32)
    xdg[t, 0:own_rows] = dec_own
    gain_row = gain[...]
    gain_t[...] = jnp.broadcast_to(gain_row, (CHUNK, gain_row.shape[1])).T
    pl.semaphore_wait(barrier, n + 1)

    def x_copies(sems, where, owner):
        copies = [remote(xdg.at[owner], xdg.at[owner], sems, chunks, where)]
        for i in range(chunks):
            src = x_pre.at[:, chunk(i)] if owner is t else xg.at[owner, i]
            copies.append(remote(src, xg.at[owner, i], sems, i, where))
        return copies

    over = x_copies(xy_sem, {"tp": across}, t)
    beside = x_copies(xc_sem, {"tp": mate}, t)
    passed = x_copies(xf_sem, {"tp": mate}, across)
    for i in range(chunks + 1):
        over[i].start()
    for i in range(chunks + 1):
        beside[i].start()
    load_wo.start()
    load_dk.start()
    load_dv.start()
    share_wo = remote(w_out, wo.at[core], wo_sem, 0, {"tp": mate})
    share_wo.start()

    def pass_on(i):
        over[i].wait_recv()
        passed[i].start()

    def normalize(tokens, axis, scale):
        mean_square = jnp.sum(tokens * tokens, axis=axis, keepdims=True) * (1.0 / tokens.shape[axis])
        return tokens * lax.rsqrt(mean_square + EPSILON) * scale

    pass_on(0)
    pass_on(1)
    beside[0].wait_recv()
    passed[0].wait_recv()
    dec_normed = normalize(jnp.concatenate([xdg[p] for p in range(4)], axis=1), 1, gain_row)

    prefix = pre_lens[0]
    prefix_bias = jnp.where(lanes((1, cached)) < prefix, 0.0, MASKED)
    tri = (CHUNK, CHUNK)
    causal_bias = jnp.where(lanes(tri) <= lax.broadcasted_iota(jnp.int32, tri, 0), 0.0, MASKED)

    def project(i):
        beside[i + 1].wait_recv()
        passed[i + 1].wait_recv()
        load_x[i].wait()
        tokens = jnp.concatenate([xg[p, i].astype(F32) for p in range(4)], axis=0)
        normed = normalize(tokens, 0, gain_t[...]).astype(BF16)
        if i == 0:
            extra = jnp.concatenate([dec_normed] * (CHUNK // DEC_ROWS), axis=0).T.astype(BF16)
            normed = jnp.concatenate([normed, extra], axis=1)
            load_wq.wait()
        return [dot(wq[m], normed) for m in range(3)]

    def attend(i, query):
        seen = cached + (i + 1) * CHUNK
        parts = []
        for head in range(4):
            low, high = WINDOWS[head]
            q = head_lanes(query, head)
            scores = dot(q, kall[low:high, 0:seen])
            pieces = [scores[:, :cached] + prefix_bias]
            if i > 0:
                pieces.append(scores[:, cached : seen - CHUNK])
            pieces.append(scores[:, seen - CHUNK :] + causal_bias)
            scores = jnp.concatenate(pieces, axis=1)
            top = jnp.max(scores, axis=-1, keepdims=True)
            weights = jnp.exp2((scores - top) * EXP_SCALE)
            total = jnp.sum(weights, axis=-1, keepdims=True)
            parts.append(dot_nt(weights.astype(BF16), vall[low:high, 0:seen]) / total)
        att[core, chunk(i)] = join_heads(parts).astype(BF16)

    att_copies = [
        remote(att.at[core, chunk(i)], att.at[core, chunk(i)], a_sem, i, {"tp": mate}) for i in range(chunks)
    ]
    attd_copy = remote(attd.at[core], attd.at[core], a_sem, chunks, {"tp": mate})
    out_copies = [remote(psend.at[chunk(i)], precv.at[chunk(i)], o_sem, i, {"tp": across}) for i in range(chunks)]
    outd_copy = remote(pdsend, pdrecv, o_sem, chunks, {"tp": across})

    def out_terms(a, to):
        return dot(a[0], wsel[to, 0]) + dot(a[1], wsel[to, 1])

    def out_project(i, with_dec):
        att_copies[i].wait_recv()
        a = [att[c, chunk(i)] for c in range(2)]
        if with_dec:
            attd_copy.wait_recv()
            d = [attd[c] for c in range(2)]
            a = [
                jnp.concatenate([a[c], jnp.concatenate([d[c], d[c]], axis=0).astype(BF16)], axis=0)
                for c in range(2)
            ]
        sent = out_terms(a, 1 - half)
        psend[chunk(i)] = sent[:CHUNK].astype(BF16)
        out_copies[i].start()
        if with_dec:
            pdsend[...] = sent[CHUNK : CHUNK + DEC_ROWS]
            outd_copy.start()
        kept = out_terms(a, half)
        own[chunk(i)] = kept[:CHUNK]
        if with_dec:
            ownd[...] = kept[CHUNK : CHUNK + DEC_ROWS]

    def finish(i):
        out_copies[i].wait_recv()
        out_pre[:, chunk(i)] = (own[chunk(i)] + precv[chunk(i)].astype(F32)).T.astype(BF16)

    def q_copy(k):
        return remote(qg.at[me], qg.at[me], q_sem, k, {"req": lax.rem(me + k, n)})

    def p_copy(k):
        to = lax.rem(me + k, n)
        return remote(part.at[to], pr.at[me], p_sem, k, {"req": to})

    def decode_partials():
        each(n, lambda k: q_copy(k).wait_recv())
        load_dk.wait()
        load_dv.wait()
        queries = qg[...].reshape(n * DEC_ROWS, width).astype(BF16)
        lens = dec_lens[...].astype(F32)
        grid = (n * DEC_ROWS, lens.shape[1])
        row = lax.broadcasted_iota(jnp.int32, grid, 0)
        place = lax.rem(row, DEC_ROWS)
        request = lax.div(row, DEC_ROWS) * own_rows + place
        real = place < own_rows
        column = lanes(grid)
        start = jnp.sum(jnp.where(real & (column < request), lens, 0.0), axis=-1, keepdims=True)
        end = jnp.sum(jnp.where(real & (column <= request), lens, 0.0), axis=-1, keepdims=True)
        pool_row = (me * pool + lanes((1, pool))).astype(F32)
        allowed = (pool_row >= start) & (pool_row < end)
        parts = []
        stats = jnp.zeros((n * DEC_ROWS, 128), F32)
        stat_lane = lanes(stats.shape)
        for head in range(4):
            low, high = WINDOWS[head]
            scores = dot(head_lanes(queries, head), dk[low:high])
            scores = jnp.where(allowed, scores, MASKED)
            top = jnp.max(scores, axis=-1, keepdims=True)
            weights = jnp.where(allowed, jnp.exp2((scores - top) * EXP_SCALE), 0.0)
            total = jnp.sum(weights, axis=-1, keepdims=True)
            parts.append(dot_nt(weights.astype(BF16), dv[low:high]))
            stats = jnp.where(stat_lane == head, top, jnp.where(stat_lane == 4 + head, total, stats))
        part[:, :, 0:width] = join_heads(parts).reshape(n, DEC_ROWS, width)
        part[:, :, 384:512] = stats.reshape(n, DEC_ROWS, 128)
        each(n, lambda k: p_copy(k).start())
        pr[me] = part[me]

    def decode_combine(q, k, v):
        each(n, lambda j: p_copy(j).wait_recv())
        sums = pr[:, :, 0:width]
        stats = pr[:, :, 384:512]
        tops, totals, selves, factors = [], [], [], []
        product = q * k
        lane = lanes(product.shape)
        for head in range(4):
            inside = (lane >= head * HD) & (lane < (head + 1) * HD)
            self_score = jnp.sum(jnp.where(inside, product, 0.0), axis=-1, keepdims=True)
            local = stats[:, :, head : head + 1]
            top = jnp.maximum(jnp.max(local, axis=0), self_score)
            factor = jnp.exp2((local - top[None]) * EXP_SCALE)
            self_weight = jnp.exp2((self_score - top) * EXP_SCALE)
            totals.append(jnp.sum(factor * stats[:, :, 4 + head : 5 + head], axis=0) + self_weight)
            selves.append(self_weight.astype(BF16).astype(F32))
            factors.append(factor)
        mixed = jnp.sum(spread(factors, sums.shape) * sums, axis=0)
        mixed = mixed + spread(selves, v.shape) * v
        attd[core] = (mixed / spread(totals, v.shape)).astype(BF16).astype(F32)
        attd_copy.start()

    for i in range(chunks):
        q, k, v = project(i)
        at = pl.ds(cached + i * CHUNK, CHUNK)
        kall[:, at] = k[:, :CHUNK].astype(BF16)
        vall[:, at] = v[:, :CHUNK].astype(BF16)
        if i == 0:
            q_own, k_own, v_own = (a[:, CHUNK:].T[:DEC_ROWS].astype(BF16).astype(F32) for a in (q, k, v))
            qg[me] = q_own
            each(n, lambda j: q_copy(j).start())
            load_pk.wait()
            load_pv.wait()
        if i + 1 < chunks:
            pass_on(i + 2)
        attend(i, q[:, :CHUNK].T.astype(BF16))
        att_copies[i].start()
        if i == 0:
            load_wo.wait()
            share_wo.wait_recv()
            for c in range(2):

                @pl.when(core == c)
                def _():
                    for to in range(2):
                        first = (2 * to + c) * width
                        for r in range(2):
                            wsel[to, r] = wo[r, :, first : first + width]

            decode_partials()
        if i == chunks - 2:
            decode_combine(q_own, k_own, v_own)
        if i > 0:
            out_project(i - 1, False)
    out_project(chunks - 1, True)
    for i in range(chunks):
        finish(i)
    outd_copy.wait_recv()
    out_dec[...] = (ownd[...] + pdrecv[...])[:own_rows].astype(BF16)

    for copy in over + beside + passed + [share_wo] + att_copies + [attd_copy] + out_copies + [outd_copy]:
        copy.wait_send()
    each(n, lambda k: q_copy(k).wait_send())
    each(n, lambda k: p_copy(k).wait_send())


def body(n, x_pre, x_dec, norm_gain, w_qkv, w_out, pre_keys, pre_values, pre_lens, dec_keys, dec_values, dec_lens):
    rows, width = x_pre.shape
    cached, pool = pre_keys.shape[0], dec_keys.shape[0]
    chunks = rows // CHUNK
    hbm = pl.BlockSpec(memory_space=pl.ANY)
    vmem = pl.BlockSpec(memory_space=pltpu.VMEM)
    smem = pl.BlockSpec(memory_space=pltpu.SMEM)
    dma = pltpu.SemaphoreType.DMA
    out_pre, out_dec = pl.pallas_call(
        functools.partial(kernel, n),
        out_shape=(jax.ShapeDtypeStruct((width, rows), BF16), jax.ShapeDtypeStruct(x_dec.shape, BF16)),
        in_specs=[hbm, vmem, vmem, hbm, hbm, hbm, hbm, smem, hbm, hbm, vmem],
        out_specs=(vmem, vmem),
        scratch_shapes=[
            pltpu.VMEM((4, chunks, width, CHUNK), BF16),
            pltpu.VMEM((4, DEC_ROWS, width), F32),
            pltpu.VMEM((norm_gain.shape[0], CHUNK), F32),
            pltpu.VMEM((3, width, w_qkv.shape[1]), BF16),
            pltpu.VMEM((2,) + w_out.shape, BF16),
            pltpu.VMEM((2, 2, width, width), BF16),
            pltpu.VMEM((width, cached + rows), BF16),
            pltpu.VMEM((width, cached + rows), BF16),
            pltpu.VMEM((width, pool), BF16),
            pltpu.VMEM((width, pool), BF16),
            pltpu.VMEM((n, DEC_ROWS, width), F32),
            pltpu.VMEM((n, DEC_ROWS, 512), F32),
            pltpu.VMEM((n, DEC_ROWS, 512), F32),
            pltpu.VMEM((2, rows, width), BF16),
            pltpu.VMEM((2, DEC_ROWS, width), F32),
            pltpu.VMEM((rows, width), F32),
            pltpu.VMEM((rows, width), BF16),
            pltpu.VMEM((rows, width), BF16),
            pltpu.VMEM((DEC_ROWS, width), F32),
            pltpu.VMEM((DEC_ROWS, width), F32),
            pltpu.VMEM((DEC_ROWS, width), F32),
            dma((6 + chunks,)),
            dma((2, chunks + 1)),
            dma((2, chunks + 1)),
            dma((2, chunks + 1)),
            dma((2, 1)),
            dma((2, n)),
            dma((2, n)),
            dma((2, chunks + 1)),
            dma((2, chunks + 1)),
        ],
        compiler_params=pltpu.CompilerParams(
            collective_id=0, has_side_effects=True, vmem_limit_bytes=60 * 1024 * 1024
        ),
        cost_estimate=pl.CostEstimate(flops=4_000_000_000, bytes_accessed=6_000_000, transcendentals=2_000_000),
    )(
        x_pre.T,
        x_dec,
        norm_gain.reshape(1, -1),
        jnp.swapaxes(w_qkv, 1, 2),
        w_out,
        pre_keys.T,
        pre_values.T,
        pre_lens,
        dec_keys.T,
        dec_values.T,
        dec_lens.reshape(1, -1),
    )
    return out_pre.T, out_dec


def solution(mesh):
    return jax.shard_map(
        functools.partial(body, mesh.shape["req"]),
        mesh=mesh,
        in_specs=(
            P("req", "tp"),
            P("req", "tp"),
            P(),
            P(None, None, "tp"),
            P("tp", None),
            P("req", "tp"),
            P("req", "tp"),
            P("req"),
            P("req", "tp"),
            P("req", "tp"),
            P(),
        ),
        out_specs=(P("req", "tp"), P("req", "tp")),
        check_vma=False,
    )
```

```python
import functools
import math

import jax
import jax.numpy as jnp
from jax import lax
from jax.experimental import pallas as pl
from jax.experimental.pallas import tpu as pltpu
from jax.sharding import PartitionSpec as P

HD = 80
EPSILON = 1e-06
MASKED = -1e30
CHUNK = 128
DEC_ROWS = 8
EXP_SCALE = math.log2(math.e) / math.sqrt(HD)
WINDOWS = ((0, 128), (0, 256), (128, 256), (128, 320))
F32, BF16 = jnp.float32, jnp.bfloat16


def lanes(shape, start=0):
    return lax.broadcasted_iota(jnp.int32, shape, len(shape) - 1) + start


def head_lanes(block, head):
    low, high = WINDOWS[head]
    part = block[:, low:high]
    lane = lanes(part.shape, low)
    return jnp.where((lane >= head * HD) & (lane < (head + 1) * HD), part, 0.0)


def join_heads(parts):
    lane = lanes((parts[0].shape[0], 128))
    first = jnp.where(lane < HD, parts[0], parts[1][:, :128])
    second = jnp.where(
        lane < 2 * HD - 128, parts[1][:, 128:], jnp.where(lane < 3 * HD - 128, parts[2], parts[3][:, :128])
    )
    return jnp.concatenate([first, second, parts[3][:, 128:]], axis=1)


def spread(columns, shape):
    lane = lanes(shape)
    out = jnp.broadcast_to(columns[3], shape)
    for head in (2, 1, 0):
        out = jnp.where(lane < (head + 1) * HD, columns[head], out)
    return out


def dot(a, b):
    return jnp.dot(a, b, preferred_element_type=F32)


def dot_nt(a, b):
    return lax.dot_general(a, b, (((1,), (1,)), ((), ())), preferred_element_type=F32)


def each(count, step):
    if count <= 16:
        for k in range(1, count):
            step(k)
    else:

        def loop(k, carry):
            step(k)
            return carry

        lax.fori_loop(1, count, loop, 0)


def kernel(
    n,
    x_pre,
    x_dec,
    gain,
    w_qkv,
    w_out,
    pre_keys,
    pre_values,
    pre_lens,
    dec_keys,
    dec_values,
    dec_lens,
    out_pre,
    out_dec,
    xg,
    xdg,
    gain_t,
    wq,
    wo,
    wsel,
    kall,
    vall,
    dk,
    dv,
    qg,
    part,
    pr,
    att,
    attd,
    own,
    psend,
    precv,
    ownd,
    pdsend,
    pdrecv,
    load_sem,
    xy_sem,
    xc_sem,
    xf_sem,
    wo_sem,
    q_sem,
    p_sem,
    a_sem,
    o_sem,
):
    width, rows = x_pre.shape
    cached = pre_keys.shape[1]
    pool = dec_keys.shape[1]
    own_rows = x_dec.shape[0]
    chunks = rows // CHUNK
    me = lax.axis_index("req")
    t = lax.axis_index("tp")
    core = lax.rem(t, 2)
    half = lax.div(t, 2)
    mate = t + 1 - 2 * core
    across = lax.rem(t + 2, 4)

    def remote(src, dst, sems, at, where):
        return pltpu.make_async_remote_copy(
            src_ref=src,
            dst_ref=dst,
            send_sem=sems.at[0, at],
            recv_sem=sems.at[1, at],
            device_id=where,
            device_id_type=pl.DeviceIdType.MESH,
        )

    def chunk(i):
        return pl.ds(i * CHUNK, CHUNK)

    load_x = [
        pltpu.make_async_copy(x_pre.at[:, chunk(i)], xg.at[t, i], load_sem.at[6 + i]) for i in range(chunks)
    ]
    load_wq = pltpu.make_async_copy(w_qkv, wq, load_sem.at[1])
    load_pk = pltpu.make_async_copy(pre_keys, kall.at[:, pl.ds(0, cached)], load_sem.at[2])
    load_pv = pltpu.make_async_copy(pre_values, vall.at[:, pl.ds(0, cached)], load_sem.at[3])
    load_dk = pltpu.make_async_copy(dec_keys, dk, load_sem.at[4])
    load_dv = pltpu.make_async_copy(dec_values, dv, load_sem.at[5])
    load_wo = pltpu.make_async_copy(w_out, wo.at[core], load_sem.at[0])
    for i in range(chunks):
        load_x[i].start()
    load_wq.start()
    load_pk.start()
    load_pv.start()

    barrier = pltpu.get_barrier_semaphore()
    for peer in (mate, across):
        pl.semaphore_signal(barrier, inc=1, device_id={"tp": peer}, device_id_type=pl.DeviceIdType.MESH)

    def greet(k):
        pl.semaphore_signal(
            barrier, inc=1, device_id={"req": lax.rem(me + k, n)}, device_id_type=pl.DeviceIdType.MESH
        )

    each(n, greet)
    dec_own = x_dec[...].astype(F32)
    xdg[t] = jnp.zeros((DEC_ROWS, width), F32)
    xdg[t, 0:own_rows] = dec_own
    gain_row = gain[...].reshape(1, gain.shape[0])
    gain_t[...] = jnp.broadcast_to(gain_row, (CHUNK, gain_row.shape[1])).T
    pl.semaphore_wait(barrier, n + 1)

    def x_copies(sems, where, owner):
        copies = [remote(xdg.at[owner], xdg.at[owner], sems, chunks, where)]
        for i in range(chunks):
            src = x_pre.at[:, chunk(i)] if owner is t else xg.at[owner, i]
            copies.append(remote(src, xg.at[owner, i], sems, i, where))
        return copies

    over = x_copies(xy_sem, {"tp": across}, t)
    beside = x_copies(xc_sem, {"tp": mate}, t)
    passed = x_copies(xf_sem, {"tp": mate}, across)
    for i in range(chunks + 1):
        over[i].start()
    for i in range(chunks + 1):
        beside[i].start()
    load_wo.start()
    load_dk.start()
    load_dv.start()
    share_wo = remote(w_out, wo.at[core], wo_sem, 0, {"tp": mate})

    def pass_on(i):
        over[i].wait_recv()
        passed[i].start()

    def normalize(tokens, axis, scale):
        mean_square = jnp.sum(tokens * tokens, axis=axis, keepdims=True) * (1.0 / tokens.shape[axis])
        return tokens * lax.rsqrt(mean_square + EPSILON) * scale

    pass_on(0)
    pass_on(1)
    beside[0].wait_recv()
    passed[0].wait_recv()
    dec_normed = normalize(jnp.concatenate([xdg[p] for p in range(4)], axis=1), 1, gain_row)

    prefix = pre_lens[0]
    prefix_bias = jnp.where(lanes((1, cached)) < prefix, 0.0, MASKED)
    tri = (CHUNK, CHUNK)
    causal_bias = jnp.where(lanes(tri) <= lax.broadcasted_iota(jnp.int32, tri, 0), 0.0, MASKED)

    def project(i):
        beside[i + 1].wait_recv()
        passed[i + 1].wait_recv()
        load_x[i].wait()
        tokens = jnp.concatenate([xg[p, i].astype(F32) for p in range(4)], axis=0)
        normed = normalize(tokens, 0, gain_t[...]).astype(BF16)
        if i == 0:
            extra = jnp.concatenate([dec_normed] * (CHUNK // DEC_ROWS), axis=0).T.astype(BF16)
            normed = jnp.concatenate([normed, extra], axis=1)
            load_wq.wait()
        return [dot(wq[m], normed) for m in range(3)]

    def attend(i, query):
        seen = cached + (i + 1) * CHUNK
        parts = []
        for head in range(4):
            low, high = WINDOWS[head]
            q = head_lanes(query, head)
            scores = dot(q, kall[low:high, 0:seen])
            pieces = [scores[:, :cached] + prefix_bias]
            if i > 0:
                pieces.append(scores[:, cached : seen - CHUNK])
            pieces.append(scores[:, seen - CHUNK :] + causal_bias)
            scores = jnp.concatenate(pieces, axis=1)
            top = jnp.max(scores, axis=-1, keepdims=True)
            weights = jnp.exp2((scores - top) * EXP_SCALE)
            total = jnp.sum(weights, axis=-1, keepdims=True)
            parts.append(dot_nt(weights.astype(BF16), vall[low:high, 0:seen]) / total)
        att[core, chunk(i)] = join_heads(parts).astype(BF16)

    att_copies = [
        remote(att.at[core, chunk(i)], att.at[core, chunk(i)], a_sem, i, {"tp": mate}) for i in range(chunks)
    ]
    attd_copy = remote(attd.at[core], attd.at[core], a_sem, chunks, {"tp": mate})
    out_copies = [remote(psend.at[chunk(i)], precv.at[chunk(i)], o_sem, i, {"tp": across}) for i in range(chunks)]
    outd_copy = remote(pdsend, pdrecv, o_sem, chunks, {"tp": across})

    def out_terms(a, to):
        return dot(a[0], wsel[to, 0]) + dot(a[1], wsel[to, 1])

    def out_project(i, with_dec):
        att_copies[i].wait_recv()
        a = [att[c, chunk(i)] for c in range(2)]
        if with_dec:
            attd_copy.wait_recv()
            d = [attd[c] for c in range(2)]
            a = [
                jnp.concatenate([a[c], jnp.concatenate([d[c], d[c]], axis=0).astype(BF16)], axis=0)
                for c in range(2)
            ]
        sent = out_terms(a, 1 - half)
        psend[chunk(i)] = sent[:CHUNK].astype(BF16)
        out_copies[i].start()
        if with_dec:
            pdsend[...] = sent[CHUNK : CHUNK + DEC_ROWS]
            outd_copy.start()
        kept = out_terms(a, half)
        own[chunk(i)] = kept[:CHUNK]
        if with_dec:
            ownd[...] = kept[CHUNK : CHUNK + DEC_ROWS]

    def finish(i):
        out_copies[i].wait_recv()
        out_pre[:, chunk(i)] = (own[chunk(i)] + precv[chunk(i)].astype(F32)).T.astype(BF16)

    def q_copy(k):
        return remote(qg.at[me], qg.at[me], q_sem, k, {"req": lax.rem(me + k, n)})

    def p_copy(k):
        to = lax.rem(me + k, n)
        return remote(part.at[to], pr.at[me], p_sem, k, {"req": to})

    def decode_partials():
        each(n, lambda k: q_copy(k).wait_recv())
        load_dk.wait()
        load_dv.wait()
        queries = qg[...].reshape(n * DEC_ROWS, width).astype(BF16)
        lens = dec_lens[...].astype(F32)
        grid = (n * DEC_ROWS, lens.shape[1])
        row = lax.broadcasted_iota(jnp.int32, grid, 0)
        place = lax.rem(row, DEC_ROWS)
        request = lax.div(row, DEC_ROWS) * own_rows + place
        real = place < own_rows
        column = lanes(grid)
        start = jnp.sum(jnp.where(real & (column < request), lens, 0.0), axis=-1, keepdims=True)
        end = jnp.sum(jnp.where(real & (column <= request), lens, 0.0), axis=-1, keepdims=True)
        pool_row = (me * pool + lanes((1, pool))).astype(F32)
        allowed = (pool_row >= start) & (pool_row < end)
        parts = []
        stats = jnp.zeros((n * DEC_ROWS, 128), F32)
        stat_lane = lanes(stats.shape)
        for head in range(4):
            low, high = WINDOWS[head]
            scores = dot(head_lanes(queries, head), dk[low:high])
            scores = jnp.where(allowed, scores, MASKED)
            top = jnp.max(scores, axis=-1, keepdims=True)
            weights = jnp.where(allowed, jnp.exp2((scores - top) * EXP_SCALE), 0.0)
            total = jnp.sum(weights, axis=-1, keepdims=True)
            parts.append(dot_nt(weights.astype(BF16), dv[low:high]))
            stats = jnp.where(stat_lane == head, top, jnp.where(stat_lane == 4 + head, total, stats))
        part[:, :, 0:width] = join_heads(parts).reshape(n, DEC_ROWS, width)
        part[:, :, 384:512] = stats.reshape(n, DEC_ROWS, 128)
        each(n, lambda k: p_copy(k).start())
        pr[me] = part[me]

    def decode_combine(q, k, v):
        each(n, lambda j: p_copy(j).wait_recv())
        sums = pr[:, :, 0:width]
        stats = pr[:, :, 384:512]
        tops, totals, selves, factors = [], [], [], []
        product = q * k
        lane = lanes(product.shape)
        for head in range(4):
            inside = (lane >= head * HD) & (lane < (head + 1) * HD)
            self_score = jnp.sum(jnp.where(inside, product, 0.0), axis=-1, keepdims=True)
            local = stats[:, :, head : head + 1]
            top = jnp.maximum(jnp.max(local, axis=0), self_score)
            factor = jnp.exp2((local - top[None]) * EXP_SCALE)
            self_weight = jnp.exp2((self_score - top) * EXP_SCALE)
            totals.append(jnp.sum(factor * stats[:, :, 4 + head : 5 + head], axis=0) + self_weight)
            selves.append(self_weight.astype(BF16).astype(F32))
            factors.append(factor)
        mixed = jnp.sum(spread(factors, sums.shape) * sums, axis=0)
        mixed = mixed + spread(selves, v.shape) * v
        attd[core] = (mixed / spread(totals, v.shape)).astype(BF16).astype(F32)
        attd_copy.start()

    for i in range(chunks):
        q, k, v = project(i)
        at = pl.ds(cached + i * CHUNK, CHUNK)
        kall[:, at] = k[:, :CHUNK].astype(BF16)
        vall[:, at] = v[:, :CHUNK].astype(BF16)
        if i == 0:
            q_own, k_own, v_own = (a[:, CHUNK:].T[:DEC_ROWS].astype(BF16).astype(F32) for a in (q, k, v))
            qg[me] = q_own
            each(n, lambda j: q_copy(j).start())
            load_pk.wait()
            load_pv.wait()
        if i + 1 < chunks:
            pass_on(i + 2)
        if i == 0:
            share_wo.start()
        attend(i, q[:, :CHUNK].T.astype(BF16))
        att_copies[i].start()
        if i == 1:
            load_wo.wait()
            share_wo.wait_recv()
            for c in range(2):

                @pl.when(core == c)
                def _():
                    for to in range(2):
                        first = (2 * to + c) * width
                        for r in range(2):
                            wsel[to, r] = wo[r, :, first : first + width]

            decode_partials()
        if i == chunks - 1:
            decode_combine(q_own, k_own, v_own)
        if i > 0:
            out_project(i - 1, False)
    out_project(chunks - 1, True)
    for i in range(chunks):
        finish(i)
    outd_copy.wait_recv()
    out_dec[...] = (ownd[...] + pdrecv[...])[:own_rows].astype(BF16)

    for copy in over + beside + passed + [share_wo] + att_copies + [attd_copy] + out_copies + [outd_copy]:
        copy.wait_send()
    each(n, lambda k: q_copy(k).wait_send())
    each(n, lambda k: p_copy(k).wait_send())


def body(n, x_pre, x_dec, norm_gain, w_qkv, w_out, pre_keys, pre_values, pre_lens, dec_keys, dec_values, dec_lens):
    rows, width = x_pre.shape
    cached, pool = pre_keys.shape[0], dec_keys.shape[0]
    chunks = rows // CHUNK
    hbm = pl.BlockSpec(memory_space=pl.ANY)
    vmem = pl.BlockSpec(memory_space=pltpu.VMEM)
    smem = pl.BlockSpec(memory_space=pltpu.SMEM)
    dma = pltpu.SemaphoreType.DMA
    out_pre, out_dec = pl.pallas_call(
        functools.partial(kernel, n),
        out_shape=(jax.ShapeDtypeStruct((width, rows), BF16), jax.ShapeDtypeStruct(x_dec.shape, BF16)),
        in_specs=[hbm, vmem, vmem, hbm, hbm, hbm, hbm, smem, hbm, hbm, vmem],
        out_specs=(vmem, vmem),
        scratch_shapes=[
            pltpu.VMEM((4, chunks, width, CHUNK), BF16),
            pltpu.VMEM((4, DEC_ROWS, width), F32),
            pltpu.VMEM((norm_gain.shape[0], CHUNK), F32),
            pltpu.VMEM((3, width, w_qkv.shape[1]), BF16),
            pltpu.VMEM((2,) + w_out.shape, BF16),
            pltpu.VMEM((2, 2, width, width), BF16),
            pltpu.VMEM((width, cached + rows), BF16),
            pltpu.VMEM((width, cached + rows), BF16),
            pltpu.VMEM((width, pool), BF16),
            pltpu.VMEM((width, pool), BF16),
            pltpu.VMEM((n, DEC_ROWS, width), F32),
            pltpu.VMEM((n, DEC_ROWS, 512), F32),
            pltpu.VMEM((n, DEC_ROWS, 512), F32),
            pltpu.VMEM((2, rows, width), BF16),
            pltpu.VMEM((2, DEC_ROWS, width), F32),
            pltpu.VMEM((rows, width), F32),
            pltpu.VMEM((rows, width), BF16),
            pltpu.VMEM((rows, width), BF16),
            pltpu.VMEM((DEC_ROWS, width), F32),
            pltpu.VMEM((DEC_ROWS, width), F32),
            pltpu.VMEM((DEC_ROWS, width), F32),
            dma((6 + chunks,)),
            dma((2, chunks + 1)),
            dma((2, chunks + 1)),
            dma((2, chunks + 1)),
            dma((2, 1)),
            dma((2, n)),
            dma((2, n)),
            dma((2, chunks + 1)),
            dma((2, chunks + 1)),
        ],
        compiler_params=pltpu.CompilerParams(
            collective_id=0, has_side_effects=True, vmem_limit_bytes=60 * 1024 * 1024
        ),
        cost_estimate=pl.CostEstimate(flops=4_000_000_000, bytes_accessed=6_000_000, transcendentals=2_000_000),
    )(
        x_pre.T,
        x_dec,
        norm_gain,
        jnp.swapaxes(w_qkv, 1, 2),
        w_out,
        pre_keys.T,
        pre_values.T,
        pre_lens,
        dec_keys.T,
        dec_values.T,
        dec_lens.reshape(1, -1),
    )
    return out_pre.T, out_dec


def solution(mesh):
    return jax.shard_map(
        functools.partial(body, mesh.shape["req"]),
        mesh=mesh,
        in_specs=(
            P("req", "tp"),
            P("req", "tp"),
            P(),
            P(None, None, "tp"),
            P("tp", None),
            P("req", "tp"),
            P("req", "tp"),
            P("req"),
            P("req", "tp"),
            P("req", "tp"),
            P(),
        ),
        out_specs=(P("req", "tp"), P("req", "tp")),
        check_vma=False,
    )
```
